32 devices in a mesh: lat: 4 (over z), lon: 8 (over y, x, core).
Axes of the slice: x: 2, y: 2, z: 4, core: 2. Of those that a mesh axis runs over, the one named last changes fastest.
Arguments:
- mesh_nodes: bfloat16 [16384, 512], P(('lat', 'lon')), may hold values from -6 to 6
- norm_gain: float32 [512], replicated, may hold values from 0.5 to 1.5
- w_query: bfloat16 [512, 512], replicated, may hold values from -0.25 to 0.25
- w_node_kv: bfloat16 [512, 1024], replicated, may hold values from -0.25 to 0.25
- obs_rows: bfloat16 [16384, 256], P(('lat', 'lon')), may hold values from -82 to 82
- w_obs_kv: bfloat16 [256, 1024], replicated, may hold values from -0.375 to 0.375
- obs_owner: int32 [16384, 1], P(('lat', 'lon')), may hold values from 0 to 31; in each aligned block of 512 rows (0 to 511, 512 to 1023, ...) at most 32 rows name the same one
- neighbours: int32 [16384, 32], P(('lat', 'lon')), may hold values from 0 to 1023
- neighbour_mask: int32 [16384, 32], P(('lat', 'lon')), may hold values 0 or 1
- disk_tokens: bfloat16 [1024, 5, 256], P(('lat', 'lon')), may hold values from -6 to 6
- w_disk_kv: bfloat16 [256, 1024], replicated, may hold values from -0.375 to 0.375
- disk_start: int32 [5], replicated, may hold values from 0 to 7
- disk_extent: int32 [5], replicated, may hold values from 2 to 4
- w_out: bfloat16 [512, 512], replicated, may hold values from -0.25 to 0.25
Outputs:
- updated: bfloat16 [16384, 512], P(('lat', 'lon'))
The draws below stay inside these ranges and needn't reach their ends.
Inputs may be any that keep to these rules, and one draw needn't show every extreme that they name: `obs_owner`: in the rows of one device, no owner is named more than 32 times, a bound that some block reaches.
All inputs are finite; a program needn't handle non-finite values. No bound on the sum of `neighbour_mask` on one device may be relied on, other than what follows from the above.
Results may differ from the reference program's by a relative error of at most 0.0039.
The reference program's roundings to bfloat16 on the way count: a program that leaves them out, or rounds other values in their place, can miss the bound.
Values may be sent and summed in bfloat16 or wider, within the bound.
A program may use at most 128 MiB of HBM per device.

```python
import math
import jax
import jax.numpy as jnp
import numpy as np
from jax import lax

D = 512
HEADS = 8
F_OBS = 256
F_DISK = 256
NEIGH = 32
DISKS = 5
DISK_TOK = 1024
NODE_DEV = 512
OBS_DEV = 512
CAP = 32
SLOTS = 1024
NODES = 16384
OBS = 16384
N_LAT = 4
N_LON = 8
DEVICES = 32


def draw_obs_rows(key, part):
    first_key = jax.random.fold_in(jax.random.fold_in(key, 11), 0)
    base = jax.random.truncated_normal(first_key, -4.0, 4.0, (OBS, F_OBS), jnp.float32)
    return base.astype(jnp.bfloat16)


def draw_disk_extent(key, part):
    least_span = N_LON // 4
    most_span = N_LON // 2
    spans = jax.random.randint(jax.random.fold_in(key, 23), (DISKS,), least_span, most_span + 1)
    spans = spans.at[0].set(most_span).at[1].set(least_span)
    return spans.astype(jnp.int32)


def with_ends(drawn, rng, smallest, high):
    longest = drawn.shape.index(max(drawn.shape))
    spots = []
    for shift in (0, 1):
        where = [jax.random.randint(jax.random.fold_in(rng, axis), (), 0, length) for axis, length in enumerate(drawn.shape)]
        where[longest] = (where[longest] + shift) % drawn.shape[longest]
        spots.append(tuple(where))
    return drawn.at[spots[0]].set(smallest).at[spots[1]].set(high)


def block_scale(stream_key, dims, pieces, least, high):
    factor_of, own = 1.0, jax.random.fold_in(stream_key, 6)
    for dim, parts in pieces:
        draws = jnp.exp(jax.random.uniform(jax.random.fold_in(own, dim), (parts,), jnp.float32, least / len(pieces), high / len(pieces)))
        factor_of = factor_of * jnp.repeat(draws, dims[dim] // parts).reshape([-1 if axis == dim else 1 for axis in range(len(dims))])
    return factor_of


def assign_block(stream_key, own, number, rows, count, top, bound, slope):
    order = jax.random.permutation(stream_key, count)
    heavy_load, ordinary = load_shares(count, rows * top, bound, slope, True), load_shares(count, rows * top, bound, slope, False)
    places = jnp.arange(count)

    def named(tallies, turn):
        used = int((tallies > 0).sum())
        fixed = max(1, used // 4)
        passed = fixed + (places - fixed + turn * (used - fixed)) % max(1, count - fixed)
        return jnp.zeros((count,), jnp.int32).at[order[jnp.where(places < fixed, places, passed)]].set(jnp.asarray(tallies, jnp.int32))

    tallies = jnp.where(number % 4 == 0, named(heavy_load, number // 4), named(ordinary, number - number // 4 - 1))
    mixed = jax.random.permutation(jax.random.fold_in(own, 3), count)
    giver, sink = mixed[0:count // 2 * 2:2], mixed[1:count // 2 * 2:2]
    slack = jnp.minimum(tallies[giver] - 1, bound - tallies[sink]) // 2
    slack = jnp.where((giver == order[0]) | (sink == order[0]) | (tallies[sink] == 0), 0, jnp.maximum(slack, 0))
    passed = jax.random.randint(jax.random.fold_in(own, 4), (count // 2,), 0, 1 << 20) % (slack + 1)
    tallies = tallies.at[giver].add(-passed).at[sink].add(passed)
    labels = jnp.searchsorted(jnp.cumsum(tallies), jnp.arange(rows * top), side="right").astype(jnp.int32)
    listing = labels.reshape(top, rows).T
    listing = listing[jax.random.permutation(jax.random.fold_in(own, 1), rows)]
    turn = jax.random.randint(jax.random.fold_in(own, 2), (rows, 1), 0, top)
    return jnp.take_along_axis(listing, (jnp.arange(top)[None, :] + turn) % top, axis=1)


def load_shares(count, total, reach, lean, full):
    weights = [(1 << 20) // math.isqrt(standing ** lean) + 1 for standing in range(1, count + 1)]
    largest = reach if full else min(reach, max(-(-total // count), total * weights[0] // sum(weights)))
    least = 1 if total - largest >= count - 1 else 0
    counts, rest = [largest] + [least] * (count - 1), total - largest - least * (count - 1)
    while rest > 0:
        movable = [i for i in range(1, count) if counts[i] < largest] or [i for i in range(1, count) if counts[i] < reach]
        pool, budget = sum([weights[i] for i in movable]), rest
        for i in movable:
            extra = min(reach - counts[i], max(1, budget * weights[i] // pool), rest)
            counts[i] = counts[i] + extra
            rest = rest - extra
    return np.array(counts)


def gaussian(own_key, dims, scale, bound, cuts=(), kind=jnp.bfloat16):
    drawn = scale * jax.random.normal(own_key, dims, jnp.float32)
    if cuts:
        drawn = drawn * block_scale(own_key, dims, cuts, -0.22, 0.18)
    return jnp.clip(drawn, -bound, bound).astype(kind)


def setup_inputs(seed: int = 0) -> dict:
    splits = jax.random.split(jax.random.key(seed), 15)
    mesh_nodes = gaussian(splits[0], (NODES, D), 1.0, 6.0, ((0, 32),))
    norm_gain = jnp.clip(1.0 + 0.1 * jax.random.normal(splits[1], (D,), jnp.float32), 0.5, 1.5)
    w_query = gaussian(splits[2], (D, D), D ** -0.5, 0.25)
    w_node_kv = gaussian(splits[3], (D, 2 * D), D ** -0.5, 0.25)
    obs_rows = draw_obs_rows(jax.random.fold_in(splits[14], 71), 0)
    w_obs_kv = gaussian(splits[5], (F_OBS, 2 * D), F_OBS ** -0.5, 0.375)
    obs_owner_keys = jax.random.split(jax.random.fold_in(splits[6], 1), OBS // OBS_DEV)
    obs_owner_turns = jax.random.permutation(jax.random.fold_in(splits[6], 3), OBS // OBS_DEV)
    obs_owner = jax.vmap(lambda own, number: assign_block(jax.random.fold_in(splits[6], 2), own, number, OBS_DEV, DEVICES, 1, CAP, 2))(obs_owner_keys, obs_owner_turns).reshape((OBS, 1))
    neighbours = with_ends(jax.random.randint(splits[7], (NODES, NEIGH), 0, SLOTS), jax.random.fold_in(splits[7], 1), 0, SLOTS - 1).astype(jnp.int32)
    neighbour_mask = with_ends((jax.random.randint(splits[8], (NODES, NEIGH), 0, 4) < 3).astype(jnp.int32), jax.random.fold_in(splits[8], 1), 0, 1)
    disk_tokens = gaussian(splits[9], (DISK_TOK, DISKS, F_DISK), 1.0, 6.0, ((0, 32),))
    w_disk_kv = gaussian(splits[10], (F_DISK, 2 * D), F_DISK ** -0.5, 0.375)
    disk_start = with_ends(jax.random.randint(splits[11], (DISKS,), 0, N_LON), jax.random.fold_in(splits[11], 1), 0, N_LON - 1).astype(jnp.int32)
    disk_extent = draw_disk_extent(jax.random.fold_in(splits[14], 71), 0)
    w_out = gaussian(splits[13], (D, D), D ** -0.5, 0.25)
    return {"mesh_nodes": mesh_nodes, "norm_gain": norm_gain, "w_query": w_query, "w_node_kv": w_node_kv, "obs_rows": obs_rows, "w_obs_kv": w_obs_kv, "obs_owner": obs_owner, "neighbours": neighbours, "neighbour_mask": neighbour_mask, "disk_tokens": disk_tokens, "w_disk_kv": w_disk_kv, "disk_start": disk_start, "disk_extent": disk_extent, "w_out": w_out}


def split_heads(packed, head_count):
    width = packed.shape[-1] // 2
    head_width = width // head_count
    leading = packed.shape[:-1]
    return (packed[..., :width].reshape(leading + (head_count, head_width)), packed[..., width:].reshape(leading + (head_count, head_width)))

def rounded(values):
    return lax.optimization_barrier(values.astype(jnp.bfloat16)).astype(jnp.float32)

def reference(mesh_nodes, norm_gain, w_query, w_node_kv, obs_rows, w_obs_kv, obs_owner, neighbours, neighbour_mask, disk_tokens, w_disk_kv, disk_start, disk_extent, w_out):
    device_count = N_LAT * N_LON
    head_width = D // HEADS
    node_values = mesh_nodes.astype(jnp.float32)
    inverse = lax.rsqrt(lax.optimization_barrier(jnp.mean(node_values * node_values, axis=1, keepdims=True)) + 1e-06)
    normed = (node_values * inverse * norm_gain).astype(jnp.bfloat16)
    query_all = (jnp.dot(normed, w_query, preferred_element_type=jnp.float32) * head_width ** (-0.5)).astype(jnp.bfloat16)
    self_all = jnp.dot(normed, w_node_kv, preferred_element_type=jnp.float32).astype(jnp.bfloat16)
    obs_kv = jnp.dot(obs_rows, w_obs_kv, preferred_element_type=jnp.float32).astype(jnp.bfloat16)
    disk_kv = jnp.einsum('tkf,fe->kte', disk_tokens.astype(jnp.float32), w_disk_kv.astype(jnp.float32)).astype(jnp.bfloat16)
    disk_keys, disk_values = split_heads(disk_kv, HEADS)
    flat_values = disk_values.reshape(DISKS * DISK_TOK, HEADS, head_width).astype(jnp.float32)
    device_ids = jnp.arange(device_count, dtype=jnp.int32)
    obs_dest = obs_owner[:, 0].reshape(device_count, OBS_DEV)
    dest_hot = (obs_dest[:, :, None] == device_ids[None, None, :]).astype(jnp.int32)
    obs_rank = lax.optimization_barrier(jnp.sum((jnp.cumsum(dest_hot, axis=1) - dest_hot) * dest_hot, axis=2))
    source_ids = jnp.broadcast_to(device_ids[:, None], (device_count, OBS_DEV))
    target = (obs_dest * SLOTS + source_ids * CAP + obs_rank).reshape(-1).astype(jnp.int32)
    slot_table = jnp.full((device_count * SLOTS,), -1, jnp.int32).at[target].set(jnp.arange(OBS, dtype=jnp.int32))
    visible_all = jnp.mod(device_ids[:, None] % N_LON - disk_start[None, :], N_LON) < disk_extent[None, :]

    def one_device(device):
        query_heads = lax.dynamic_slice_in_dim(query_all, device * NODE_DEV, NODE_DEV, 0).reshape(NODE_DEV, HEADS, head_width).astype(jnp.float32)
        self_kv = lax.dynamic_slice_in_dim(self_all, device * NODE_DEV, NODE_DEV, 0).astype(jnp.float32)
        self_keys, self_values = split_heads(self_kv, HEADS)
        slot_ids = lax.dynamic_slice_in_dim(slot_table, device * SLOTS, SLOTS, 0)
        filled = slot_ids >= 0
        slot_kv = jnp.where(filled[:, None], obs_kv[jnp.maximum(slot_ids, 0)], jnp.zeros((), jnp.bfloat16))
        listed = lax.dynamic_slice_in_dim(neighbours, device * NODE_DEV, NODE_DEV, 0)
        mark_values = lax.dynamic_slice_in_dim(neighbour_mask, device * NODE_DEV, NODE_DEV, 0)
        valid_slot = (mark_values > 0) & filled[listed]
        near_keys, near_values = split_heads(slot_kv[listed].astype(jnp.float32), HEADS)
        self_scores = lax.optimization_barrier(jnp.sum(query_heads * self_keys, axis=2))
        near_scores = jnp.einsum('nhd,nehd->nhe', query_heads, near_keys)
        near_scores = jnp.where(valid_slot[:, None, :], near_scores, -jnp.inf)
        visible = visible_all[device]
        score_list = []
        for disk_index in range(DISKS):
            score_list.append(lax.cond(visible[disk_index], lambda keys: jnp.einsum('nhd,thd->nht', query_heads, keys), lambda keys: jnp.full((NODE_DEV, HEADS, DISK_TOK), -jnp.inf, query_heads.dtype), disk_keys[disk_index].astype(jnp.float32)))
        disk_scores = jnp.concatenate(score_list, axis=2)
        row_top = jnp.maximum(jnp.maximum(self_scores, lax.optimization_barrier(jnp.max(near_scores, axis=2))), lax.optimization_barrier(jnp.max(disk_scores, axis=2)))
        self_weight = jnp.exp(self_scores - row_top)
        near_weight = jnp.exp(near_scores - row_top[:, :, None])
        disk_weight = jnp.exp(disk_scores - row_top[:, :, None])
        denominator = self_weight + lax.optimization_barrier(jnp.sum(near_weight, axis=2)) + lax.optimization_barrier(jnp.sum(disk_weight, axis=2))
        summed = rounded(self_weight)[:, :, None] * self_values
        summed = summed + jnp.einsum('nhe,nehd->nhd', rounded(near_weight), near_values)
        summed = summed + jnp.einsum('nht,thd->nhd', rounded(disk_weight), flat_values)
        return (summed / denominator[:, :, None]).reshape(NODE_DEV, D).astype(jnp.bfloat16)
    attended = lax.map(one_device, device_ids).reshape(NODES, D)
    mixed_rows = jnp.dot(attended, w_out, preferred_element_type=jnp.float32)
    return (node_values + mixed_rows).astype(jnp.bfloat16)
```

```python
import jax
import jax.numpy as jnp
from jax import lax
from jax.experimental import pallas as pl
from jax.experimental.pallas import tpu as pltpu
from jax.sharding import PartitionSpec as P

HEADS = 8
LANES = 128
EMPTY = 1024.0
NO_ENTRY = -1e30
NT = (((1,), (1,)), ((), ()))
VMEM_BYTES = 56 * 1024 * 1024


def lower_lanes(shape):
    return lax.broadcasted_iota(jnp.int32, shape, len(shape) - 1) < LANES // 2


def project_nodes(mesh_ref, gain_ref, w_query_ref, w_node_ref, q_ref, acc_ref, top_ref):
    rows, width = mesh_ref.shape
    values = mesh_ref[...].astype(jnp.float32)
    inverse = lax.rsqrt(jnp.mean(values * values, axis=1, keepdims=True) + 1e-06)
    normed = (values * inverse * gain_ref[...]).astype(jnp.bfloat16)
    scale = (width // HEADS) ** (-0.5)
    low = lower_lanes((rows, LANES))
    for pair in range(HEADS // 2):
        cut = pl.ds(pair * LANES, LANES)
        cut_v = pl.ds(width + pair * LANES, LANES)
        query = jnp.dot(normed, w_query_ref[:, cut], preferred_element_type=jnp.float32) * scale
        query = query.astype(jnp.bfloat16).astype(jnp.float32)
        key = jnp.dot(normed, w_node_ref[:, cut], preferred_element_type=jnp.float32)
        key = key.astype(jnp.bfloat16).astype(jnp.float32)
        value = jnp.dot(normed, w_node_ref[:, cut_v], preferred_element_type=jnp.float32)
        value = value.astype(jnp.bfloat16).astype(jnp.float32)
        product = query * key
        for half in range(2):
            mine = low if half == 0 else jnp.logical_not(low)
            head = 2 * pair + half
            q_ref[head] = jnp.where(mine, query, 0.0).astype(jnp.bfloat16)
            score = jnp.sum(jnp.where(mine, product, 0.0), axis=1, keepdims=True)
            top_ref[head] = jnp.broadcast_to(score, (rows, LANES))
            acc_ref[head] = jnp.where(mine, value, 1.0)


def count_entries(listed_ref, counts_ref):
    rows, slots = counts_ref.shape
    entries = listed_ref.shape[1]
    step = 32

    @pl.loop(0, rows // step)
    def _(tile):
        cut = pl.ds(pl.multiple_of(tile * step, step), step)
        listed = listed_ref[cut, :]
        ids = lax.broadcasted_iota(jnp.int32, (step, slots), 1)
        counts = jnp.zeros((step, slots), jnp.float32)
        for entry in range(entries):
            counts = counts + jnp.where(listed[:, entry : entry + 1] == ids, 1.0, 0.0)
        counts_ref[cut, :] = counts


def project_keys(rows, w_ref, k_ref, v_ref):
    width = w_ref.shape[1] // 2
    wide = 2 * LANES
    low = lower_lanes((rows.shape[0], LANES))
    for part in range(width // wide):
        keys = jnp.dot(
            rows, w_ref[:, part * wide : (part + 1) * wide], preferred_element_type=jnp.float32
        ).astype(jnp.bfloat16)
        values = jnp.dot(
            rows,
            w_ref[:, width + part * wide : width + (part + 1) * wide],
            preferred_element_type=jnp.float32,
        )
        for sub in range(2):
            pair = 2 * part + sub
            k_ref[pair] = keys[:, sub * LANES : (sub + 1) * LANES]
            value = values[:, sub * LANES : (sub + 1) * LANES]
            v_ref[2 * pair] = jnp.where(low, value, 1.0).astype(jnp.bfloat16)
            v_ref[2 * pair + 1] = jnp.where(low, 1.0, value).astype(jnp.bfloat16)


def absorb(q_ref, k_ref, v_ref, acc_ref, top_ref, bias_ref=None):
    rows = q_ref.shape[1]
    keys = k_ref.shape[1]
    step = min(256, rows)

    @pl.loop(0, HEADS // 2)
    def _(pair):
        for half in range(2):
            head = 2 * pair + half
            for start in range(0, rows, step):
                cut = pl.ds(start, step)
                scores = lax.dot_general(
                    q_ref[head, cut, :], k_ref[pair], NT, preferred_element_type=jnp.float32
                )
                if bias_ref is not None:
                    scores = scores + bias_ref[cut, :]
                old_top = top_ref[head, cut, :]
                new_top = jnp.maximum(old_top, jnp.max(scores, axis=1, keepdims=True))
                shift = jnp.concatenate([new_top] * (keys // LANES), axis=1)
                weights = jnp.exp(scores - shift).astype(jnp.bfloat16)
                summed = jnp.dot(weights, v_ref[head], preferred_element_type=jnp.float32)
                acc_ref[head, cut, :] = acc_ref[head, cut, :] * jnp.exp(old_top - new_top) + summed
                top_ref[head, cut, :] = new_top


def finish(mesh_ref, w_out_ref, acc_ref, out_ref, joined_ref):
    rows = mesh_ref.shape[0]
    low = lower_lanes((rows, LANES))
    for pair in range(HEADS // 2):
        even, odd = acc_ref[2 * pair], acc_ref[2 * pair + 1]
        total = pltpu.roll(jnp.where(low, odd, even), LANES // 2, 1)
        joined_ref[:, pl.ds(pair * LANES, LANES)] = (jnp.where(low, even, odd) / total).astype(
            jnp.bfloat16
        )
    mixed = jnp.dot(joined_ref[...], w_out_ref[...], preferred_element_type=jnp.float32)
    out_ref[...] = (mesh_ref[...].astype(jnp.float32) + mixed).astype(jnp.bfloat16)


def slot_bias(rows_ref, bias_ref, counts_ref):
    slots, width = rows_ref.shape
    first = (lax.broadcasted_iota(jnp.int32, (8, width), 1) == 0).astype(jnp.bfloat16)
    marks = lax.dot_general(first, rows_ref[...], NT, preferred_element_type=jnp.float32)
    filled = marks[0:1, :] < EMPTY / 2
    counts = counts_ref[...]
    bias_ref[...] = jnp.where((counts > 0.0) & filled, jnp.log(counts), NO_ENTRY)


def node_kernel(
    mesh_ref, gain_ref, w_query_ref, w_node_ref, listed_ref, q_ref, acc_ref, top_ref, counts_ref
):
    project_nodes(mesh_ref, gain_ref, w_query_ref, w_node_ref, q_ref, acc_ref, top_ref)
    count_entries(listed_ref, counts_ref)


def attend_kernel(
    visible_ref,
    mesh_ref,
    q_ref,
    acc_in_ref,
    top_in_ref,
    counts_ref,
    slot_rows_ref,
    w_obs_ref,
    tokens_ref,
    w_disk_ref,
    w_out_ref,
    out_ref,
    acc_ref,
    top_ref,
    k_ref,
    v_ref,
    bias_ref,
    joined_ref,
):
    acc_ref[...] = acc_in_ref[...]
    top_ref[...] = top_in_ref[...]
    slot_bias(slot_rows_ref, bias_ref, counts_ref)
    project_keys(slot_rows_ref[...], w_obs_ref, k_ref, v_ref)
    absorb(q_ref, k_ref, v_ref, acc_ref, top_ref, bias_ref)

    @pl.loop(0, tokens_ref.shape[0])
    def _(disk):
        @pl.when(visible_ref[disk] > 0)
        def _():
            project_keys(tokens_ref[disk], w_disk_ref, k_ref, v_ref)
            absorb(q_ref, k_ref, v_ref, acc_ref, top_ref)

    finish(mesh_ref, w_out_ref, acc_ref, out_ref, joined_ref)


def local(
    mesh_nodes,
    norm_gain,
    w_query,
    w_node_kv,
    obs_rows,
    w_obs_kv,
    obs_owner,
    neighbours,
    neighbour_mask,
    disk_tokens,
    w_disk_kv,
    disk_start,
    disk_extent,
    w_out,
):
    node_count, width = mesh_nodes.shape
    lon_count = lax.axis_size("lon")
    device_count = lax.axis_size("lat") * lon_count
    visible = (jnp.mod(lax.axis_index("lon") - disk_start, lon_count) < disk_extent).astype(
        jnp.int32
    )
    tokens = lax.all_gather(
        jnp.transpose(disk_tokens, (1, 0, 2)), ("lat", "lon"), axis=1, tiled=True
    )

    obs_count, row_width = obs_rows.shape
    capacity = 2 * obs_count // device_count
    slot_count = device_count * capacity
    obs_dest = obs_owner[:, 0]
    obs_ids = jnp.arange(obs_count, dtype=jnp.int32)
    same_owner = obs_dest[:, None] == obs_dest[None, :]
    earlier = obs_ids[None, :] < obs_ids[:, None]
    obs_rank = jnp.sum((same_owner & earlier).astype(jnp.int32), axis=1)
    obs_slot = obs_dest * capacity + obs_rank
    placed = jnp.arange(slot_count, dtype=jnp.int32)[:, None] == obs_slot[None, :]
    send_rows = jnp.dot(placed.astype(jnp.bfloat16), obs_rows, preferred_element_type=jnp.float32)
    send_rows = jnp.where(jnp.any(placed, axis=1, keepdims=True), send_rows, EMPTY)
    slot_rows = lax.all_to_all(
        send_rows.astype(jnp.bfloat16).reshape(device_count, capacity, row_width),
        ("lat", "lon"),
        split_axis=0,
        concat_axis=0,
        tiled=True,
    ).reshape(slot_count, row_width)

    listed = jnp.where(neighbour_mask > 0, neighbours, -1)
    vmem = pl.BlockSpec(memory_space=pltpu.VMEM)
    smem = pl.BlockSpec(memory_space=pltpu.SMEM)
    state = (HEADS, node_count, LANES)
    q, acc, top, counts = pl.pallas_call(
        node_kernel,
        out_shape=(
            jax.ShapeDtypeStruct(state, jnp.bfloat16),
            jax.ShapeDtypeStruct(state, jnp.float32),
            jax.ShapeDtypeStruct(state, jnp.float32),
            jax.ShapeDtypeStruct((node_count, slot_count), jnp.float32),
        ),
        in_specs=[vmem] * 5,
        out_specs=(vmem,) * 4,
        compiler_params=pltpu.CompilerParams(vmem_limit_bytes=VMEM_BYTES),
        name="nodes",
    )(mesh_nodes, norm_gain.reshape(1, width), w_query, w_node_kv, listed)
    keys = max(tokens.shape[1], slot_count)
    return pl.pallas_call(
        attend_kernel,
        out_shape=jax.ShapeDtypeStruct((node_count, width), jnp.bfloat16),
        in_specs=[smem] + [vmem] * 10,
        out_specs=vmem,
        scratch_shapes=[
            pltpu.VMEM(state, jnp.float32),
            pltpu.VMEM(state, jnp.float32),
            pltpu.VMEM((HEADS // 2, keys, LANES), jnp.bfloat16),
            pltpu.VMEM((HEADS, keys, LANES), jnp.bfloat16),
            pltpu.VMEM((node_count, slot_count), jnp.float32),
            pltpu.VMEM((node_count, width), jnp.bfloat16),
        ],
        compiler_params=pltpu.CompilerParams(vmem_limit_bytes=VMEM_BYTES),
        name="attend",
    )(
        visible,
        mesh_nodes,
        q,
        acc,
        top,
        counts,
        slot_rows,
        w_obs_kv,
        tokens,
        w_disk_kv,
        w_out,
    )


def solution(mesh):
    rows = P(("lat", "lon"), None)
    return jax.shard_map(
        local,
        mesh=mesh,
        in_specs=(
            rows,
            P(),
            P(),
            P(),
            rows,
            P(),
            rows,
            rows,
            rows,
            P(("lat", "lon"), None, None),
            P(),
            P(),
            P(),
            P(),
        ),
        out_specs=rows,
        check_vma=False,
    )
```

```python
import functools

import jax
import jax.numpy as jnp
from jax import lax
from jax.experimental import pallas as pl
from jax.experimental.pallas import tpu as pltpu
from jax.sharding import PartitionSpec as P

HEADS = 8
LANES = 128
EMPTY = 1024.0
NO_ENTRY = -1e30
NT = (((1,), (1,)), ((), ()))
VMEM_BYTES = 56 * 1024 * 1024


def lower_lanes(shape):
    return lax.broadcasted_iota(jnp.int32, shape, len(shape) - 1) < LANES // 2


def project_nodes(mesh_ref, gain_ref, w_query_ref, w_node_ref, q_ref, acc_ref, top_ref):
    rows, width = mesh_ref.shape
    values = mesh_ref[...].astype(jnp.float32)
    inverse = lax.rsqrt(jnp.mean(values * values, axis=1, keepdims=True) + 1e-06)
    normed = (values * inverse * gain_ref[...]).astype(jnp.bfloat16)
    scale = (width // HEADS) ** (-0.5)
    low = lower_lanes((rows, LANES))
    for pair in range(HEADS // 2):
        cut = pl.ds(pair * LANES, LANES)
        cut_v = pl.ds(width + pair * LANES, LANES)
        query = jnp.dot(normed, w_query_ref[:, cut], preferred_element_type=jnp.float32) * scale
        query = query.astype(jnp.bfloat16).astype(jnp.float32)
        key = jnp.dot(normed, w_node_ref[:, cut], preferred_element_type=jnp.float32)
        key = key.astype(jnp.bfloat16).astype(jnp.float32)
        value = jnp.dot(normed, w_node_ref[:, cut_v], preferred_element_type=jnp.float32)
        value = value.astype(jnp.bfloat16).astype(jnp.float32)
        product = query * key
        for half in range(2):
            mine = low if half == 0 else jnp.logical_not(low)
            head = 2 * pair + half
            q_ref[head] = jnp.where(mine, query, 0.0).astype(jnp.bfloat16)
            score = jnp.sum(jnp.where(mine, product, 0.0), axis=1, keepdims=True)
            top_ref[head] = jnp.broadcast_to(score, (rows, LANES))
            acc_ref[head] = jnp.where(mine, value, 1.0)


def count_entries(listed_ref, counts_ref):
    rows, slots = counts_ref.shape
    entries = listed_ref.shape[1]
    step = 32

    @pl.loop(0, rows // step)
    def _(tile):
        cut = pl.ds(pl.multiple_of(tile * step, step), step)
        listed = listed_ref[cut, :]
        ids = lax.broadcasted_iota(jnp.int32, (step, slots), 1)
        counts = jnp.zeros((step, slots), jnp.float32)
        for entry in range(entries):
            counts = counts + jnp.where(listed[:, entry : entry + 1] == ids, 1.0, 0.0)
        counts_ref[cut, :] = counts


def project_keys(rows, w_ref, k_ref, v_ref):
    width = w_ref.shape[1] // 2
    wide = 2 * LANES
    low = lower_lanes((rows.shape[0], LANES))
    for part in range(width // wide):
        keys = jnp.dot(
            rows, w_ref[:, part * wide : (part + 1) * wide], preferred_element_type=jnp.float32
        ).astype(jnp.bfloat16)
        values = jnp.dot(
            rows,
            w_ref[:, width + part * wide : width + (part + 1) * wide],
            preferred_element_type=jnp.float32,
        )
        for sub in range(2):
            pair = 2 * part + sub
            k_ref[pair] = keys[:, sub * LANES : (sub + 1) * LANES]
            value = values[:, sub * LANES : (sub + 1) * LANES]
            v_ref[2 * pair] = jnp.where(low, value, 1.0).astype(jnp.bfloat16)
            v_ref[2 * pair + 1] = jnp.where(low, 1.0, value).astype(jnp.bfloat16)


def absorb(q_ref, k_ref, v_ref, acc_ref, top_ref, bias_ref=None):
    rows = q_ref.shape[1]
    keys = k_ref.shape[1]
    step = min(256, rows)

    @pl.loop(0, HEADS // 2)
    def _(pair):
        for half in range(2):
            head = 2 * pair + half
            for start in range(0, rows, step):
                cut = pl.ds(start, step)
                scores = lax.dot_general(
                    q_ref[head, cut, :], k_ref[pair], NT, preferred_element_type=jnp.float32
                )
                if bias_ref is not None:
                    scores = scores + bias_ref[cut, :]
                old_top = top_ref[head, cut, :]
                new_top = jnp.maximum(old_top, jnp.max(scores, axis=1, keepdims=True))
                shift = jnp.concatenate([new_top] * (keys // LANES), axis=1)
                weights = jnp.exp(scores - shift).astype(jnp.bfloat16)
                summed = jnp.dot(weights, v_ref[head], preferred_element_type=jnp.float32)
                acc_ref[head, cut, :] = acc_ref[head, cut, :] * jnp.exp(old_top - new_top) + summed
                top_ref[head, cut, :] = new_top


def finish(mesh_ref, w_out_ref, acc_ref, out_ref, joined_ref):
    rows = mesh_ref.shape[0]
    low = lower_lanes((rows, LANES))
    for pair in range(HEADS // 2):
        even, odd = acc_ref[2 * pair], acc_ref[2 * pair + 1]
        total = pltpu.roll(jnp.where(low, odd, even), LANES // 2, 1)
        joined_ref[:, pl.ds(pair * LANES, LANES)] = (jnp.where(low, even, odd) / total).astype(
            jnp.bfloat16
        )
    mixed = jnp.dot(joined_ref[...], w_out_ref[...], preferred_element_type=jnp.float32)
    out_ref[...] = (mesh_ref[...].astype(jnp.float32) + mixed).astype(jnp.bfloat16)


def slot_bias(rows_ref, bias_ref, counts_ref):
    slots, width = rows_ref.shape
    first = (lax.broadcasted_iota(jnp.int32, (8, width), 1) == 0).astype(jnp.bfloat16)
    marks = lax.dot_general(first, rows_ref[...], NT, preferred_element_type=jnp.float32)
    filled = marks[0:1, :] < EMPTY / 2
    counts = counts_ref[...]
    bias_ref[...] = jnp.where((counts > 0.0) & filled, jnp.log(counts), NO_ENTRY)


def place_rows(owner_col_ref, owner_row_ref, obs_ref, send_ref):
    devices, capacity, width = send_ref.shape
    count = obs_ref.shape[0]
    square = (count, count)
    before = lax.broadcasted_iota(jnp.int32, square, 0) < lax.broadcasted_iota(jnp.int32, square, 1)
    same = owner_col_ref[...] == owner_row_ref[...]
    rank = jnp.sum(jnp.where(same & before, 1.0, 0.0), axis=0, keepdims=True).astype(jnp.int32)
    slot = owner_row_ref[...] * capacity + rank
    table = (devices * capacity, count)
    placed = jnp.where(lax.broadcasted_iota(jnp.int32, table, 0) == slot, 1.0, 0.0)
    rows = jnp.dot(placed.astype(jnp.bfloat16), obs_ref[...], preferred_element_type=jnp.float32)
    filled = jnp.max(placed, axis=1, keepdims=True) > 0.0
    rows = jnp.where(filled, rows, EMPTY)
    send_ref[...] = rows.reshape(devices, capacity, width).astype(jnp.bfloat16)


def flat_rows(block):
    lead, rows, width = block.shape
    if rows % 16 == 0:
        return block.reshape(lead * rows, width)
    return block.astype(jnp.float32).reshape(lead * rows, width).astype(jnp.bfloat16)


def exchange_kernel(
    lat_count,
    lon_count,
    mesh_ref,
    gain_ref,
    w_query_ref,
    w_node_ref,
    neighbours_ref,
    mask_ref,
    owner_col_ref,
    owner_row_ref,
    obs_ref,
    w_obs_ref,
    shard_ref,
    q_ref,
    acc_ref,
    top_ref,
    tokens_ref,
    send_ref,
    got_ref,
    rows_ref,
    listed_ref,
    counts_ref,
    bias_ref,
    k_ref,
    v_ref,
    own_sem,
    column_send,
    column_recv,
    chip_send,
    chip_recv,
    core_send,
    core_recv,
    slot_send,
    slot_recv,
):
    my_lat, my_lon = lax.axis_index("lat"), lax.axis_index("lon")
    devices = lat_count * lon_count
    chips = lon_count // 2
    chip, core = my_lon // 2, lax.rem(my_lon, 2)
    me = my_lat * lon_count + my_lon

    def place(device):
        return (device // lon_count, lax.rem(device, lon_count))

    barrier = pltpu.get_barrier_semaphore()

    @pl.loop(1, devices)
    def _(away):
        to = place(lax.rem(me + away, devices))
        pl.semaphore_signal(barrier, inc=1, device_id=to, device_id_type=pl.DeviceIdType.MESH)

    own = pltpu.make_async_copy(shard_ref, tokens_ref.at[me], own_sem)
    own.start()
    place_rows(owner_col_ref, owner_row_ref, obs_ref, send_ref)
    got_ref[me] = send_ref[me]
    pl.semaphore_wait(barrier, devices - 1)

    def push(source, block, send_sem, recv_sem, to):
        return pltpu.make_async_remote_copy(
            src_ref=source,
            dst_ref=tokens_ref.at[block],
            send_sem=send_sem,
            recv_sem=recv_sem,
            device_id=to,
            device_id_type=pl.DeviceIdType.MESH,
        )

    def back(index, away, count):
        return lax.rem(index + count - away, count)

    def column_copy(away, lat):
        block = lat * lon_count + my_lon
        to = (lax.rem(my_lat + away, lat_count), my_lon)
        return push(shard_ref, block, column_send.at[away], column_recv.at[lat], to)

    def chip_copy(source, lat_away, lat, chip_away, from_chip):
        block = lat * lon_count + 2 * from_chip + core
        to = (my_lat, 2 * lax.rem(chip + chip_away, chips) + core)
        return push(
            source,
            block,
            chip_send.at[lat_away * chips + chip_away],
            chip_recv.at[lat * chips + from_chip],
            to,
        )

    def core_copy(source, lat_away, lat, chip_away, from_chip, from_core):
        block = lat * lon_count + 2 * from_chip + from_core
        to = (my_lat, 2 * chip + 1 - core)
        return push(
            source,
            block,
            core_send.at[lat_away * chips + chip_away],
            core_recv.at[lat * chips + from_chip],
            to,
        )

    def slot_copy(away, origin):
        target = lax.rem(me + away, devices)
        return pltpu.make_async_remote_copy(
            src_ref=send_ref.at[target],
            dst_ref=got_ref.at[origin],
            send_sem=slot_send.at[away],
            recv_sem=slot_recv.at[origin],
            device_id=place(target),
            device_id_type=pl.DeviceIdType.MESH,
        )

    @pl.loop(1, lat_count)
    def _(away):
        column_copy(away, my_lat).start()

    @pl.loop(1, chips)
    def _(away):
        chip_copy(shard_ref, 0, my_lat, away, chip).start()

    core_copy(shard_ref, 0, my_lat, 0, chip, core).start()

    @pl.loop(1, devices)
    def _(away):
        slot_copy(away, me).start()

    project_nodes(mesh_ref, gain_ref, w_query_ref, w_node_ref, q_ref, acc_ref, top_ref)

    @pl.loop(1, lat_count)
    def _(lat_away):
        lat = back(my_lat, lat_away, lat_count)
        column_copy(lat_away, lat).wait_recv()
        held = tokens_ref.at[lat * lon_count + my_lon]

        @pl.loop(1, chips)
        def _(away):
            chip_copy(held, lat_away, lat, away, chip).start()

        core_copy(held, lat_away, lat, 0, chip, core).start()

    listed_ref[...] = jnp.where(mask_ref[...] > 0, neighbours_ref[...], -1)
    count_entries(listed_ref, counts_ref)

    @pl.loop(0, lat_count)
    def _(lat_away):
        lat = back(my_lat, lat_away, lat_count)

        @pl.loop(1, chips)
        def _(away):
            origin = back(chip, away, chips)
            held = tokens_ref.at[lat * lon_count + 2 * origin + core]
            chip_copy(held, lat_away, lat, away, origin).wait_recv()
            core_copy(held, lat_away, lat, away, origin, core).start()

    @pl.loop(1, devices)
    def _(away):
        slot_copy(away, back(me, away, devices)).wait_recv()

    rows_ref[...] = flat_rows(got_ref[...])
    slot_bias(rows_ref, bias_ref, counts_ref)
    project_keys(rows_ref[...], w_obs_ref, k_ref, v_ref)
    absorb(q_ref, k_ref, v_ref, acc_ref, top_ref, bias_ref)

    @pl.loop(0, lat_count)
    def _(lat_away):
        lat = back(my_lat, lat_away, lat_count)

        @pl.loop(0, chips)
        def _(away):
            origin = back(chip, away, chips)
            held = tokens_ref.at[lat * lon_count + 2 * origin + core]
            core_copy(held, lat_away, lat, away, origin, 1 - core).wait_recv()
            core_copy(held, lat_away, lat, away, origin, core).wait_send()

        @pl.loop(1, chips)
        def _(away):
            chip_copy(shard_ref, lat_away, lat, away, chip).wait_send()

    @pl.loop(1, lat_count)
    def _(away):
        column_copy(away, my_lat).wait_send()

    @pl.loop(1, devices)
    def _(away):
        slot_copy(away, me).wait_send()

    own.wait()


def attend_kernel(
    visible_ref,
    mesh_ref,
    q_ref,
    acc_in_ref,
    top_in_ref,
    tokens_ref,
    w_disk_ref,
    w_out_ref,
    out_ref,
    acc_ref,
    top_ref,
    k_ref,
    v_ref,
    joined_ref,
):
    acc_ref[...] = acc_in_ref[...]
    top_ref[...] = top_in_ref[...]

    @pl.loop(0, tokens_ref.shape[1])
    def _(disk):
        @pl.when(visible_ref[disk] > 0)
        def _():
            project_keys(flat_rows(tokens_ref[:, disk]), w_disk_ref, k_ref, v_ref)
            absorb(q_ref, k_ref, v_ref, acc_ref, top_ref)

    finish(mesh_ref, w_out_ref, acc_ref, out_ref, joined_ref)


def local(
    mesh_nodes,
    norm_gain,
    w_query,
    w_node_kv,
    obs_rows,
    w_obs_kv,
    obs_owner,
    neighbours,
    neighbour_mask,
    disk_tokens,
    w_disk_kv,
    disk_start,
    disk_extent,
    w_out,
):
    node_count, width = mesh_nodes.shape
    lon_count = lax.axis_size("lon")
    device_count = lax.axis_size("lat") * lon_count
    visible = (jnp.mod(lax.axis_index("lon") - disk_start, lon_count) < disk_extent).astype(
        jnp.int32
    )
    lat_count = lax.axis_size("lat")
    token_count, disk_count, token_width = disk_tokens.shape
    obs_count, row_width = obs_rows.shape
    capacity = 2 * obs_count // device_count
    slot_count = device_count * capacity
    vmem = pl.BlockSpec(memory_space=pltpu.VMEM)
    smem = pl.BlockSpec(memory_space=pltpu.SMEM)
    hbm = pl.BlockSpec(memory_space=pl.ANY)
    state = (HEADS, node_count, LANES)
    shard_count = lat_count * lon_count // 2
    dma = pltpu.SemaphoreType.DMA
    q, acc, top, tokens = pl.pallas_call(
        functools.partial(exchange_kernel, lat_count, lon_count),
        out_shape=(
            jax.ShapeDtypeStruct(state, jnp.bfloat16),
            jax.ShapeDtypeStruct(state, jnp.float32),
            jax.ShapeDtypeStruct(state, jnp.float32),
            jax.ShapeDtypeStruct(
                (device_count, disk_count, token_count, token_width), jnp.bfloat16
            ),
        ),
        in_specs=[vmem] * 10 + [hbm],
        out_specs=(vmem,) * 3 + (hbm,),
        scratch_shapes=[
            pltpu.VMEM((device_count, capacity, row_width), jnp.bfloat16),
            pltpu.VMEM((device_count, capacity, row_width), jnp.bfloat16),
            pltpu.VMEM((slot_count, row_width), jnp.bfloat16),
            pltpu.VMEM(neighbours.shape, jnp.int32),
            pltpu.VMEM((node_count, slot_count), jnp.float32),
            pltpu.VMEM((node_count, slot_count), jnp.float32),
            pltpu.VMEM((HEADS // 2, slot_count, LANES), jnp.bfloat16),
            pltpu.VMEM((HEADS, slot_count, LANES), jnp.bfloat16),
            dma,
            dma((lat_count,)),
            dma((lat_count,)),
            dma((shard_count,)),
            dma((shard_count,)),
            dma((shard_count,)),
            dma((shard_count,)),
            dma((device_count,)),
            dma((device_count,)),
        ],
        compiler_params=pltpu.CompilerParams(
            vmem_limit_bytes=VMEM_BYTES, collective_id=0, has_side_effects=True
        ),
        name="exchange",
    )(
        mesh_nodes,
        norm_gain.reshape(1, width),
        w_query,
        w_node_kv,
        neighbours,
        neighbour_mask,
        obs_owner,
        obs_owner.reshape(1, obs_count),
        obs_rows,
        w_obs_kv,
        jnp.transpose(disk_tokens, (1, 0, 2)),
    )
    keys = device_count * token_count
    return pl.pallas_call(
        attend_kernel,
        out_shape=jax.ShapeDtypeStruct((node_count, width), jnp.bfloat16),
        in_specs=[smem] + [vmem] * 7,
        out_specs=vmem,
        scratch_shapes=[
            pltpu.VMEM(state, jnp.float32),
            pltpu.VMEM(state, jnp.float32),
            pltpu.VMEM((HEADS // 2, keys, LANES), jnp.bfloat16),
            pltpu.VMEM((HEADS, keys, LANES), jnp.bfloat16),
            pltpu.VMEM((node_count, width), jnp.bfloat16),
        ],
        compiler_params=pltpu.CompilerParams(vmem_limit_bytes=VMEM_BYTES),
        name="attend",
    )(visible, mesh_nodes, q, acc, top, tokens, w_disk_kv, w_out)


def solution(mesh):
    rows = P(("lat", "lon"), None)
    return jax.shard_map(
        local,
        mesh=mesh,
        in_specs=(
            rows,
            P(),
            P(),
            P(),
            rows,
            P(),
            rows,
            rows,
            rows,
            P(("lat", "lon"), None, None),
            P(),
            P(),
            P(),
            P(),
        ),
        out_specs=rows,
        check_vma=False,
    )
```

```python
import functools

import jax
import jax.numpy as jnp
from jax import lax
from jax.experimental import pallas as pl
from jax.experimental.pallas import tpu as pltpu
from jax.sharding import PartitionSpec as P

HEADS = 8
LANES = 128
EMPTY = 1024.0
NO_ENTRY = -1e30
NT = (((1,), (1,)), ((), ()))
VMEM_BYTES = 56 * 1024 * 1024


def lower_lanes(shape):
    return lax.broadcasted_iota(jnp.int32, shape, len(shape) - 1) < LANES // 2


def project_nodes(mesh_ref, gain_ref, w_query_ref, w_node_ref, q_ref, acc_ref, top_ref):
    rows, width = mesh_ref.shape
    values = mesh_ref[...].astype(jnp.float32)
    inverse = lax.rsqrt(jnp.mean(values * values, axis=1, keepdims=True) + 1e-06)
    normed = (values * inverse * gain_ref[...]).astype(jnp.bfloat16)
    scale = (width // HEADS) ** (-0.5)
    low = lower_lanes((rows, LANES))
    for pair in range(HEADS // 2):
        cut = pl.ds(pair * LANES, LANES)
        cut_v = pl.ds(width + pair * LANES, LANES)
        query = jnp.dot(normed, w_query_ref[:, cut], preferred_element_type=jnp.float32) * scale
        query = query.astype(jnp.bfloat16).astype(jnp.float32)
        key = jnp.dot(normed, w_node_ref[:, cut], preferred_element_type=jnp.float32)
        key = key.astype(jnp.bfloat16).astype(jnp.float32)
        value = jnp.dot(normed, w_node_ref[:, cut_v], preferred_element_type=jnp.float32)
        value = value.astype(jnp.bfloat16).astype(jnp.float32)
        product = query * key
        for half in range(2):
            mine = low if half == 0 else jnp.logical_not(low)
            head = 2 * pair + half
            q_ref[head] = jnp.where(mine, query, 0.0).astype(jnp.bfloat16)
            score = jnp.sum(jnp.where(mine, product, 0.0), axis=1, keepdims=True)
            top_ref[head] = jnp.broadcast_to(score, (rows, LANES))
            acc_ref[head] = jnp.where(mine, value, 1.0)


def count_entries(listed, counts_ref):
    slots, nodes = counts_ref.shape
    step = 32
    listed = listed.astype(jnp.int16)

    @pl.loop(0, slots // step)
    def _(tile):
        ids = lax.broadcasted_iota(jnp.int32, (step, nodes), 0) + tile * step
        ids = ids.astype(jnp.int16)
        counts = jnp.zeros((step, nodes), jnp.int16)
        one, zero = jnp.ones((step, nodes), jnp.int16), jnp.zeros((step, nodes), jnp.int16)
        for entry in range(listed.shape[0]):
            row = jnp.broadcast_to(listed[entry : entry + 1, :], (step, nodes))
            counts = counts + jnp.where(row == ids, one, zero)
        cut = pl.ds(pl.multiple_of(tile * step, step), step)
        counts_ref[cut, :] = counts.astype(jnp.int32).astype(jnp.float32)


def project_keys(rows, w_ref, k_ref, v_ref):
    width = w_ref.shape[1] // 2
    wide = 2 * LANES
    low = lower_lanes((rows.shape[0], LANES))
    for part in range(width // wide):
        keys = jnp.dot(
            rows, w_ref[:, part * wide : (part + 1) * wide], preferred_element_type=jnp.float32
        ).astype(jnp.bfloat16)
        values = jnp.dot(
            rows,
            w_ref[:, width + part * wide : width + (part + 1) * wide],
            preferred_element_type=jnp.float32,
        )
        for sub in range(2):
            pair = 2 * part + sub
            k_ref[pair] = keys[:, sub * LANES : (sub + 1) * LANES]
            value = values[:, sub * LANES : (sub + 1) * LANES]
            v_ref[2 * pair] = jnp.where(low, value, 1.0).astype(jnp.bfloat16)
            v_ref[2 * pair + 1] = jnp.where(low, 1.0, value).astype(jnp.bfloat16)


def absorb(q_ref, k_ref, v_ref, acc_ref, top_ref, bias_ref=None, first=0, last=HEADS // 2):
    rows = q_ref.shape[1]
    keys = k_ref.shape[1]
    step = min(256, rows)
    blocks = [(half, start) for half in range(2) for start in range(0, rows, step)]

    @pl.loop(first, last)
    def _(pair):
        def score(half, start):
            cut = pl.ds(start, step)
            scores = lax.dot_general(
                q_ref[2 * pair + half, cut, :],
                k_ref[pair],
                NT,
                preferred_element_type=jnp.float32,
            )
            return scores if bias_ref is None else scores + bias_ref[cut, :]

        ahead = score(*blocks[0])
        for index, (half, start) in enumerate(blocks):
            scores = ahead
            if index + 1 < len(blocks):
                ahead = score(*blocks[index + 1])
            head, cut = 2 * pair + half, pl.ds(start, step)
            old_top = top_ref[head, cut, :]
            new_top = jnp.maximum(old_top, jnp.max(scores, axis=1, keepdims=True))
            shift = jnp.concatenate([new_top] * (keys // LANES), axis=1)
            weights = jnp.exp((scores - shift).astype(jnp.bfloat16))
            summed = jnp.dot(weights, v_ref[head], preferred_element_type=jnp.float32)
            acc_ref[head, cut, :] = acc_ref[head, cut, :] * jnp.exp(old_top - new_top) + summed
            top_ref[head, cut, :] = new_top


def finish(mesh_ref, w_out_ref, acc_ref, out_ref, joined_ref):
    rows = mesh_ref.shape[0]
    low = lower_lanes((rows, LANES))
    for pair in range(HEADS // 2):
        even, odd = acc_ref[2 * pair], acc_ref[2 * pair + 1]
        total = pltpu.roll(jnp.where(low, odd, even), LANES // 2, 1)
        joined_ref[:, pl.ds(pair * LANES, LANES)] = (jnp.where(low, even, odd) / total).astype(
            jnp.bfloat16
        )
    mixed = jnp.dot(joined_ref[...], w_out_ref[...], preferred_element_type=jnp.float32)
    out_ref[...] = (mesh_ref[...].astype(jnp.float32) + mixed).astype(jnp.bfloat16)


def slot_bias(rows_ref, bias_ref, counts_ref):
    filled = rows_ref[:, 0:LANES].astype(jnp.float32)[:, 0:1] < EMPTY / 2
    counts = counts_ref[...]
    bias = jnp.where((counts > 0.0) & filled, jnp.log(counts), NO_ENTRY)
    bias_ref[...] = jnp.transpose(bias)


def place_rows(owner_row_ref, obs_ref, send_ref):
    devices, capacity, width = send_ref.shape
    count = obs_ref.shape[0]
    square = (count, count)
    before = lax.broadcasted_iota(jnp.int32, square, 0) < lax.broadcasted_iota(jnp.int32, square, 1)
    owner = jnp.broadcast_to(owner_row_ref[...].astype(jnp.float32), (8, count))
    same = jnp.transpose(owner)[:, 0:1] == owner[0:1, :]
    rank = jnp.sum(jnp.where(same & before, 1.0, 0.0), axis=0, keepdims=True).astype(jnp.int32)
    slot = owner_row_ref[...] * capacity + rank
    table = (devices * capacity, count)
    placed = jnp.where(lax.broadcasted_iota(jnp.int32, table, 0) == slot, 1.0, 0.0)
    rows = jnp.dot(placed.astype(jnp.bfloat16), obs_ref[...], preferred_element_type=jnp.float32)
    filled = jnp.max(placed, axis=1, keepdims=True) > 0.0
    rows = jnp.where(filled, rows, EMPTY)
    send_ref[...] = rows.reshape(devices, capacity, width).astype(jnp.bfloat16)


def flat_rows(block):
    lead, rows, width = block.shape
    if rows % 16 == 0:
        return block.reshape(lead * rows, width)
    return block.astype(jnp.float32).reshape(lead * rows, width).astype(jnp.bfloat16)


def exchange_kernel(
    lat_count,
    lon_count,
    mesh_ref,
    gain_ref,
    w_query_ref,
    w_node_ref,
    neighbours_ref,
    mask_ref,
    owner_row_ref,
    obs_ref,
    w_obs_ref,
    shard_ref,
    q_ref,
    acc_ref,
    top_ref,
    tokens_ref,
    send_ref,
    got_ref,
    rows_ref,
    counts_ref,
    bias_ref,
    k_ref,
    v_ref,
    own_sem,
    column_send,
    column_recv,
    chip_send,
    chip_recv,
    core_send,
    core_recv,
    slot_send,
    slot_recv,
):
    my_lat, my_lon = lax.axis_index("lat"), lax.axis_index("lon")
    devices = lat_count * lon_count
    chips = lon_count // 2
    chip, core = my_lon // 2, lax.rem(my_lon, 2)
    me = my_lat * lon_count + my_lon

    def place(device):
        return (device // lon_count, lax.rem(device, lon_count))

    barrier = pltpu.get_barrier_semaphore()

    @pl.loop(1, devices)
    def _(away):
        to = place(lax.rem(me + away, devices))
        pl.semaphore_signal(barrier, inc=1, device_id=to, device_id_type=pl.DeviceIdType.MESH)

    own = pltpu.make_async_copy(shard_ref, tokens_ref.at[me], own_sem)
    own.start()
    place_rows(owner_row_ref, obs_ref, send_ref)
    got_ref[me] = send_ref[me]
    pl.semaphore_wait(barrier, devices - 1)

    def push(source, block, send_sem, recv_sem, to):
        return pltpu.make_async_remote_copy(
            src_ref=source,
            dst_ref=tokens_ref.at[block],
            send_sem=send_sem,
            recv_sem=recv_sem,
            device_id=to,
            device_id_type=pl.DeviceIdType.MESH,
        )

    def back(index, away, count):
        return lax.rem(index + count - away, count)

    def column_copy(away, lat):
        block = lat * lon_count + my_lon
        to = (lax.rem(my_lat + away, lat_count), my_lon)
        return push(shard_ref, block, column_send.at[away], column_recv.at[lat], to)

    def chip_copy(source, lat_away, lat, chip_away, from_chip):
        block = lat * lon_count + 2 * from_chip + core
        to = (my_lat, 2 * lax.rem(chip + chip_away, chips) + core)
        return push(
            source,
            block,
            chip_send.at[lat_away * chips + chip_away],
            chip_recv.at[lat * chips + from_chip],
            to,
        )

    def core_copy(source, lat_away, lat, chip_away, from_chip, from_core):
        block = lat * lon_count + 2 * from_chip + from_core
        to = (my_lat, 2 * chip + 1 - core)
        return push(
            source,
            block,
            core_send.at[lat_away * chips + chip_away],
            core_recv.at[lat * chips + from_chip],
            to,
        )

    def slot_copy(away, origin):
        target = lax.rem(me + away, devices)
        return pltpu.make_async_remote_copy(
            src_ref=send_ref.at[target],
            dst_ref=got_ref.at[origin],
            send_sem=slot_send.at[away],
            recv_sem=slot_recv.at[origin],
            device_id=place(target),
            device_id_type=pl.DeviceIdType.MESH,
        )

    @pl.loop(1, lat_count)
    def _(away):
        column_copy(away, my_lat).start()

    @pl.loop(1, chips)
    def _(away):
        chip_copy(shard_ref, 0, my_lat, away, chip).start()

    core_copy(shard_ref, 0, my_lat, 0, chip, core).start()

    @pl.loop(1, devices)
    def _(away):
        slot_copy(away, me).start()

    project_nodes(mesh_ref, gain_ref, w_query_ref, w_node_ref, q_ref, acc_ref, top_ref)

    @pl.loop(1, lat_count)
    def _(lat_away):
        lat = back(my_lat, lat_away, lat_count)
        column_copy(lat_away, lat).wait_recv()
        held = tokens_ref.at[lat * lon_count + my_lon]

        @pl.loop(1, chips)
        def _(away):
            chip_copy(held, lat_away, lat, away, chip).start()

        core_copy(held, lat_away, lat, 0, chip, core).start()

    count_entries(jnp.where(mask_ref[...] > 0, neighbours_ref[...], -1), counts_ref)

    @pl.loop(1, devices)
    def _(away):
        slot_copy(away, back(me, away, devices)).wait_recv()

    rows_ref[...] = flat_rows(got_ref[...])
    slot_bias(rows_ref, bias_ref, counts_ref)
    project_keys(rows_ref[...], w_obs_ref, k_ref, v_ref)
    def pass_on(lat_away):
        lat = back(my_lat, lat_away, lat_count)

        @pl.loop(1, chips)
        def _(away):
            origin = back(chip, away, chips)
            held = tokens_ref.at[lat * lon_count + 2 * origin + core]
            chip_copy(held, lat_away, lat, away, origin).wait_recv()
            core_copy(held, lat_away, lat, away, origin, core).start()

    split = lat_count // 2
    absorb(q_ref, k_ref, v_ref, acc_ref, top_ref, bias_ref, 0, HEADS // 2 - 1)
    pl.loop(0, split)(pass_on)
    absorb(q_ref, k_ref, v_ref, acc_ref, top_ref, bias_ref, HEADS // 2 - 1, HEADS // 2)
    pl.loop(split, lat_count)(pass_on)

    @pl.loop(0, lat_count)
    def _(lat_away):
        lat = back(my_lat, lat_away, lat_count)

        @pl.loop(0, chips)
        def _(away):
            origin = back(chip, away, chips)
            held = tokens_ref.at[lat * lon_count + 2 * origin + core]
            core_copy(held, lat_away, lat, away, origin, 1 - core).wait_recv()
            core_copy(held, lat_away, lat, away, origin, core).wait_send()

        @pl.loop(1, chips)
        def _(away):
            chip_copy(shard_ref, lat_away, lat, away, chip).wait_send()

    @pl.loop(1, lat_count)
    def _(away):
        column_copy(away, my_lat).wait_send()

    @pl.loop(1, devices)
    def _(away):
        slot_copy(away, me).wait_send()

    own.wait()


def attend_kernel(
    lon_count,
    start_ref,
    extent_ref,
    mesh_ref,
    q_in_ref,
    acc_in_ref,
    top_in_ref,
    shards_ref,
    w_disk_ref,
    w_out_ref,
    out_ref,
    q_ref,
    acc_ref,
    top_ref,
    tokens_ref,
    k_ref,
    v_ref,
    joined_ref,
    state_sem,
    token_sem,
):
    lon = lax.axis_index("lon")
    disks = shards_ref.shape[1]

    def seen(disk):
        return lax.rem(lon - start_ref[disk] + lon_count, lon_count) < extent_ref[disk]

    def fetch(disk):
        return pltpu.make_async_copy(
            shards_ref.at[:, disk], tokens_ref.at[disk], token_sem.at[disk]
        )

    loads = [
        pltpu.make_async_copy(q_in_ref, q_ref, state_sem.at[0]),
        pltpu.make_async_copy(top_in_ref, top_ref, state_sem.at[1]),
        pltpu.make_async_copy(acc_in_ref, acc_ref, state_sem.at[2]),
    ]
    for load in loads:
        load.start()
    for disk in range(disks):

        @pl.when(seen(disk))
        def _():
            fetch(disk).start()

    for load in loads:
        load.wait()

    @pl.loop(0, disks)
    def _(disk):
        @pl.when(seen(disk))
        def _():
            fetch(disk).wait()
            project_keys(flat_rows(tokens_ref[disk]), w_disk_ref, k_ref, v_ref)
            absorb(q_ref, k_ref, v_ref, acc_ref, top_ref)

    finish(mesh_ref, w_out_ref, acc_ref, out_ref, joined_ref)


def local(
    mesh_nodes,
    norm_gain,
    w_query,
    w_node_kv,
    obs_rows,
    w_obs_kv,
    obs_owner,
    neighbours,
    neighbour_mask,
    disk_tokens,
    w_disk_kv,
    disk_start,
    disk_extent,
    w_out,
):
    node_count, width = mesh_nodes.shape
    lon_count = lax.axis_size("lon")
    device_count = lax.axis_size("lat") * lon_count
    lat_count = lax.axis_size("lat")
    token_count, disk_count, token_width = disk_tokens.shape
    obs_count, row_width = obs_rows.shape
    capacity = 2 * obs_count // device_count
    slot_count = device_count * capacity
    vmem = pl.BlockSpec(memory_space=pltpu.VMEM)
    smem = pl.BlockSpec(memory_space=pltpu.SMEM)
    hbm = pl.BlockSpec(memory_space=pl.ANY)
    state = (HEADS, node_count, LANES)
    shard_count = lat_count * lon_count // 2
    dma = pltpu.SemaphoreType.DMA
    q, acc, top, tokens = pl.pallas_call(
        functools.partial(exchange_kernel, lat_count, lon_count),
        out_shape=(
            jax.ShapeDtypeStruct(state, jnp.bfloat16),
            jax.ShapeDtypeStruct(state, jnp.float32),
            jax.ShapeDtypeStruct(state, jnp.float32),
            jax.ShapeDtypeStruct(
                (device_count, disk_count, token_count, token_width), jnp.bfloat16
            ),
        ),
        in_specs=[vmem] * 9 + [hbm],
        out_specs=(vmem,) * 3 + (hbm,),
        scratch_shapes=[
            pltpu.VMEM((device_count, capacity, row_width), jnp.bfloat16),
            pltpu.VMEM((device_count, capacity, row_width), jnp.bfloat16),
            pltpu.VMEM((slot_count, row_width), jnp.bfloat16),
            pltpu.VMEM((slot_count, node_count), jnp.float32),
            pltpu.VMEM((node_count, slot_count), jnp.float32),
            pltpu.VMEM((HEADS // 2, slot_count, LANES), jnp.bfloat16),
            pltpu.VMEM((HEADS, slot_count, LANES), jnp.bfloat16),
            dma,
            dma((lat_count,)),
            dma((lat_count,)),
            dma((shard_count,)),
            dma((shard_count,)),
            dma((shard_count,)),
            dma((shard_count,)),
            dma((device_count,)),
            dma((device_count,)),
        ],
        compiler_params=pltpu.CompilerParams(
            vmem_limit_bytes=VMEM_BYTES, collective_id=0, has_side_effects=True
        ),
        name="exchange",
    )(
        mesh_nodes,
        norm_gain.reshape(1, width),
        w_query,
        w_node_kv,
        neighbours.T,
        neighbour_mask.T,
        obs_owner.reshape(1, obs_count),
        obs_rows,
        w_obs_kv,
        jnp.transpose(disk_tokens, (1, 0, 2)),
    )
    keys = device_count * token_count
    return pl.pallas_call(
        functools.partial(attend_kernel, lon_count),
        out_shape=jax.ShapeDtypeStruct((node_count, width), jnp.bfloat16),
        in_specs=[smem] * 2 + [vmem] + [hbm] * 4 + [vmem] * 2,
        out_specs=vmem,
        scratch_shapes=[
            pltpu.VMEM(state, jnp.bfloat16),
            pltpu.VMEM(state, jnp.float32),
            pltpu.VMEM(state, jnp.float32),
            pltpu.VMEM((disk_count, device_count, token_count, token_width), jnp.bfloat16),
            pltpu.VMEM((HEADS // 2, keys, LANES), jnp.bfloat16),
            pltpu.VMEM((HEADS, keys, LANES), jnp.bfloat16),
            pltpu.VMEM((node_count, width), jnp.bfloat16),
            dma((3,)),
            dma((disk_count,)),
        ],
        compiler_params=pltpu.CompilerParams(vmem_limit_bytes=VMEM_BYTES),
        name="attend",
    )(disk_start, disk_extent, mesh_nodes, q, acc, top, tokens, w_disk_kv, w_out)


def solution(mesh):
    rows = P(("lat", "lon"), None)
    return jax.shard_map(
        local,
        mesh=mesh,
        in_specs=(
            rows,
            P(),
            P(),
            P(),
            rows,
            P(),
            rows,
            rows,
            rows,
            P(("lat", "lon"), None, None),
            P(),
            P(),
            P(),
            P(),
        ),
        out_specs=rows,
        check_vma=False,
    )
```

```python
import functools

import jax
import jax.numpy as jnp
from jax import lax
from jax.experimental import pallas as pl
from jax.experimental.pallas import tpu as pltpu
from jax.sharding import PartitionSpec as P

HEADS = 8
LANES = 128
EMPTY = 1024.0
NO_ENTRY = -1e30
NT = (((1,), (1,)), ((), ()))
VMEM_BYTES = 56 * 1024 * 1024


def lower_lanes(shape):
    return lax.broadcasted_iota(jnp.int32, shape, len(shape) - 1) < LANES // 2


def project_nodes(mesh_ref, gain_ref, w_query_ref, w_node_ref, q_ref, acc_ref, top_ref):
    rows, width = mesh_ref.shape
    values = mesh_ref[...].astype(jnp.float32)
    inverse = lax.rsqrt(jnp.mean(values * values, axis=1, keepdims=True) + 1e-06)
    normed = (values * inverse * gain_ref[...]).astype(jnp.bfloat16)
    scale = (width // HEADS) ** (-0.5)
    low = lower_lanes((rows, LANES))
    for pair in range(HEADS // 2):
        cut = pl.ds(pair * LANES, LANES)
        cut_v = pl.ds(width + pair * LANES, LANES)
        query = jnp.dot(normed, w_query_ref[:, cut], preferred_element_type=jnp.float32) * scale
        query = query.astype(jnp.bfloat16).astype(jnp.float32)
        key = jnp.dot(normed, w_node_ref[:, cut], preferred_element_type=jnp.float32)
        key = key.astype(jnp.bfloat16).astype(jnp.float32)
        value = jnp.dot(normed, w_node_ref[:, cut_v], preferred_element_type=jnp.float32)
        value = value.astype(jnp.bfloat16).astype(jnp.float32)
        product = query * key
        for half in range(2):
            mine = low if half == 0 else jnp.logical_not(low)
            head = 2 * pair + half
            q_ref[head] = jnp.where(mine, query, 0.0).astype(jnp.bfloat16)
            score = jnp.sum(jnp.where(mine, product, 0.0), axis=1, keepdims=True)
            top_ref[head] = jnp.broadcast_to(score, (rows, LANES))
            acc_ref[head] = jnp.where(mine, value, 1.0)


def count_entries(listed, counts_ref):
    slots, nodes = counts_ref.shape
    step = 32
    listed = listed.astype(jnp.int16)

    @pl.loop(0, slots // step)
    def _(tile):
        ids = lax.broadcasted_iota(jnp.int32, (step, nodes), 0) + tile * step
        ids = ids.astype(jnp.int16)
        counts = jnp.zeros((step, nodes), jnp.int16)
        one, zero = jnp.ones((step, nodes), jnp.int16), jnp.zeros((step, nodes), jnp.int16)
        for entry in range(listed.shape[0]):
            row = jnp.broadcast_to(listed[entry : entry + 1, :], (step, nodes))
            counts = counts + jnp.where(row == ids, one, zero)
        cut = pl.ds(pl.multiple_of(tile * step, step), step)
        counts_ref[cut, :] = counts.astype(jnp.int32).astype(jnp.float32)


def project_keys(rows, w_ref, k_ref, v_ref):
    width = w_ref.shape[1] // 2
    wide = 2 * LANES
    low = lower_lanes((rows.shape[0], LANES))
    for part in range(width // wide):
        keys = jnp.dot(
            rows, w_ref[:, part * wide : (part + 1) * wide], preferred_element_type=jnp.float32
        ).astype(jnp.bfloat16)
        values = jnp.dot(
            rows,
            w_ref[:, width + part * wide : width + (part + 1) * wide],
            preferred_element_type=jnp.float32,
        )
        for sub in range(2):
            pair = 2 * part + sub
            k_ref[pair] = keys[:, sub * LANES : (sub + 1) * LANES]
            value = values[:, sub * LANES : (sub + 1) * LANES]
            v_ref[2 * pair] = jnp.where(low, value, 1.0).astype(jnp.bfloat16)
            v_ref[2 * pair + 1] = jnp.where(low, 1.0, value).astype(jnp.bfloat16)


def absorb(q_ref, k_ref, v_ref, acc_ref, top_ref, bias_ref=None, penalties=(0.0,)):
    rows = q_ref.shape[1]
    keys = k_ref.shape[1]
    step = min(256, rows)
    blocks = [(half, start) for half in range(2) for start in range(0, rows, step)]

    part = keys // len(penalties)

    @pl.loop(0, HEADS // 2)
    def _(pair):
        def score(half, start):
            cut = pl.ds(start, step)
            scores = lax.dot_general(
                q_ref[2 * pair + half, cut, :],
                k_ref[pair],
                NT,
                preferred_element_type=jnp.float32,
            )
            return scores if bias_ref is None else scores + bias_ref[cut, :]

        ahead = score(*blocks[0])
        for index, (half, start) in enumerate(blocks):
            scores = ahead
            if index + 1 < len(blocks):
                ahead = score(*blocks[index + 1])
            head, cut = 2 * pair + half, pl.ds(start, step)
            old_top = top_ref[head, cut, :]
            lane_top = old_top
            for index_part, penalty in enumerate(penalties):
                part_top = scores[:, index_part * part : index_part * part + LANES]
                for at in range(index_part * part + LANES, (index_part + 1) * part, LANES):
                    part_top = jnp.maximum(part_top, scores[:, at : at + LANES])
                lane_top = jnp.maximum(lane_top, part_top - penalty)
            row_top = jnp.max(lane_top, axis=1, keepdims=True)
            new_top = jnp.maximum(old_top, row_top)
            shift = jnp.concatenate(
                [new_top + penalty for penalty in penalties for _ in range(part // LANES)], axis=1
            )
            weights = jnp.exp((scores - shift).astype(jnp.bfloat16))
            summed = jnp.dot(weights, v_ref[head], preferred_element_type=jnp.float32)
            acc_ref[head, cut, :] = acc_ref[head, cut, :] * jnp.exp(old_top - new_top) + summed
            top_ref[head, cut, :] = new_top


def finish(mesh_ref, w_out_ref, acc_ref, out_ref, joined_ref):
    rows = mesh_ref.shape[0]
    low = lower_lanes((rows, LANES))
    for pair in range(HEADS // 2):
        even, odd = acc_ref[2 * pair], acc_ref[2 * pair + 1]
        total = pltpu.roll(jnp.where(low, odd, even), LANES // 2, 1)
        joined_ref[:, pl.ds(pair * LANES, LANES)] = (jnp.where(low, even, odd) / total).astype(
            jnp.bfloat16
        )
    mixed = jnp.dot(joined_ref[...], w_out_ref[...], preferred_element_type=jnp.float32)
    out_ref[...] = (mesh_ref[...].astype(jnp.float32) + mixed).astype(jnp.bfloat16)


def slot_bias(rows_ref, bias_ref, counts_ref):
    filled = rows_ref[:, 0:LANES].astype(jnp.float32)[:, 0:1] < EMPTY / 2
    counts = counts_ref[...]
    bias = jnp.where((counts > 0.0) & filled, jnp.log(counts), NO_ENTRY)
    bias_ref[...] = jnp.transpose(bias)


def place_rows(owner_row_ref, obs_ref, send_ref):
    devices, capacity, width = send_ref.shape
    count = obs_ref.shape[0]
    square = (count, count)
    before = lax.broadcasted_iota(jnp.int32, square, 0) < lax.broadcasted_iota(jnp.int32, square, 1)
    owner = jnp.broadcast_to(owner_row_ref[...].astype(jnp.float32), (8, count))
    same = jnp.transpose(owner)[:, 0:1] == owner[0:1, :]
    rank = jnp.sum(jnp.where(same & before, 1.0, 0.0), axis=0, keepdims=True).astype(jnp.int32)
    slot = owner_row_ref[...] * capacity + rank
    table = (devices * capacity, count)
    placed = jnp.where(lax.broadcasted_iota(jnp.int32, table, 0) == slot, 1.0, 0.0)
    rows = jnp.dot(placed.astype(jnp.bfloat16), obs_ref[...], preferred_element_type=jnp.float32)
    filled = jnp.max(placed, axis=1, keepdims=True) > 0.0
    rows = jnp.where(filled, rows, EMPTY)
    send_ref[...] = rows.reshape(devices, capacity, width).astype(jnp.bfloat16)


def flat_rows(block):
    lead, rows, width = block.shape
    if rows % 16 == 0:
        return block.reshape(lead * rows, width)
    return block.astype(jnp.float32).reshape(lead * rows, width).astype(jnp.bfloat16)


def exchange_kernel(
    lat_count,
    lon_count,
    start_ref,
    extent_ref,
    mesh_ref,
    gain_ref,
    w_query_ref,
    w_node_ref,
    neighbours_ref,
    mask_ref,
    owner_row_ref,
    obs_ref,
    w_obs_ref,
    w_disk_ref,
    w_out_ref,
    shard_ref,
    out_ref,
    q_ref,
    acc_ref,
    top_ref,
    tokens_ref,
    disk_k_ref,
    disk_v_ref,
    joined_ref,
    send_ref,
    got_ref,
    rows_ref,
    counts_ref,
    bias_ref,
    k_ref,
    v_ref,
    own_sem,
    column_send,
    column_recv,
    chip_send,
    chip_recv,
    core_send,
    core_recv,
    slot_send,
    slot_recv,
):
    my_lat, my_lon = lax.axis_index("lat"), lax.axis_index("lon")
    devices = lat_count * lon_count
    chips = lon_count // 2
    chip, core = my_lon // 2, lax.rem(my_lon, 2)
    me = my_lat * lon_count + my_lon

    def place(device):
        return (device // lon_count, lax.rem(device, lon_count))

    barrier = pltpu.get_barrier_semaphore()

    @pl.loop(1, devices)
    def _(away):
        to = place(lax.rem(me + away, devices))
        pl.semaphore_signal(barrier, inc=1, device_id=to, device_id_type=pl.DeviceIdType.MESH)

    own = pltpu.make_async_copy(shard_ref, tokens_ref.at[me], own_sem)
    own.start()
    place_rows(owner_row_ref, obs_ref, send_ref)
    got_ref[me] = send_ref[me]
    pl.semaphore_wait(barrier, devices - 1)

    def push(source, block, send_sem, recv_sem, to):
        return pltpu.make_async_remote_copy(
            src_ref=source,
            dst_ref=tokens_ref.at[block],
            send_sem=send_sem,
            recv_sem=recv_sem,
            device_id=to,
            device_id_type=pl.DeviceIdType.MESH,
        )

    def back(index, away, count):
        return lax.rem(index + count - away, count)

    def column_copy(away, lat):
        block = lat * lon_count + my_lon
        to = (lax.rem(my_lat + away, lat_count), my_lon)
        return push(shard_ref, block, column_send.at[away], column_recv.at[lat], to)

    def chip_copy(source, lat_away, lat, chip_away, from_chip):
        block = lat * lon_count + 2 * from_chip + core
        to = (my_lat, 2 * lax.rem(chip + chip_away, chips) + core)
        return push(
            source,
            block,
            chip_send.at[lat_away * chips + chip_away],
            chip_recv.at[lat * chips + from_chip],
            to,
        )

    def core_copy(source, lat_away, lat, chip_away, from_chip, from_core):
        block = lat * lon_count + 2 * from_chip + from_core
        to = (my_lat, 2 * chip + 1 - core)
        return push(
            source,
            block,
            core_send.at[lat_away * chips + chip_away],
            core_recv.at[lat * chips + from_chip],
            to,
        )

    def slot_copy(away, origin):
        target = lax.rem(me + away, devices)
        return pltpu.make_async_remote_copy(
            src_ref=send_ref.at[target],
            dst_ref=got_ref.at[origin],
            send_sem=slot_send.at[away],
            recv_sem=slot_recv.at[origin],
            device_id=place(target),
            device_id_type=pl.DeviceIdType.MESH,
        )

    @pl.loop(1, lat_count)
    def _(away):
        column_copy(away, my_lat).start()

    @pl.loop(1, chips)
    def _(away):
        chip_copy(shard_ref, 0, my_lat, away, chip).start()

    core_copy(shard_ref, 0, my_lat, 0, chip, core).start()

    @pl.loop(1, devices)
    def _(away):
        slot_copy(away, me).start()

    project_nodes(mesh_ref, gain_ref, w_query_ref, w_node_ref, q_ref, acc_ref, top_ref)

    @pl.loop(1, lat_count)
    def _(lat_away):
        lat = back(my_lat, lat_away, lat_count)
        column_copy(lat_away, lat).wait_recv()
        held = tokens_ref.at[lat * lon_count + my_lon]

        @pl.loop(1, chips)
        def _(away):
            chip_copy(held, lat_away, lat, away, chip).start()

        core_copy(held, lat_away, lat, 0, chip, core).start()

    count_entries(jnp.where(mask_ref[...] > 0, neighbours_ref[...], -1), counts_ref)

    def pass_on(lat_away):
        lat = back(my_lat, lat_away, lat_count)

        @pl.loop(1, chips)
        def _(away):
            origin = back(chip, away, chips)
            held = tokens_ref.at[lat * lon_count + 2 * origin + core]
            chip_copy(held, lat_away, lat, away, origin).wait_recv()
            core_copy(held, lat_away, lat, away, origin, core).start()

    pass_on(0)

    @pl.loop(1, devices)
    def _(away):
        slot_copy(away, back(me, away, devices)).wait_recv()

    rows_ref[...] = flat_rows(got_ref[...])
    slot_bias(rows_ref, bias_ref, counts_ref)
    project_keys(rows_ref[...], w_obs_ref, k_ref, v_ref)
    absorb(q_ref, k_ref, v_ref, acc_ref, top_ref, bias_ref)
    own.wait()
    if lat_count > 1:
        pass_on(1)

    disks, token_count = shard_ref.shape[0], shard_ref.shape[1]
    part = lon_count * token_count
    penalties = []
    for disk in range(disks):
        ahead = lax.rem(my_lon - start_ref[disk] + lon_count, lon_count)
        penalties.append(jnp.where(ahead < extent_ref[disk], 0.0, -NO_ENTRY))

    @pl.loop(0, lat_count)
    def _(lat_away):
        lat = back(my_lat, lat_away, lat_count)

        @pl.loop(0, chips)
        def _(away):
            origin = back(chip, away, chips)
            held = tokens_ref.at[lat * lon_count + 2 * origin + core]
            core_copy(held, lat_away, lat, away, origin, 1 - core).wait_recv()

        for disk in range(disks):
            cut = pl.ds(disk * part, part)
            rows = flat_rows(tokens_ref[pl.ds(lat * lon_count, lon_count), disk])
            project_keys(rows, w_disk_ref, disk_k_ref.at[:, cut], disk_v_ref.at[:, cut])
        absorb(q_ref, disk_k_ref, disk_v_ref, acc_ref, top_ref, None, penalties)

        @pl.when(lat_away + 2 < lat_count)
        def _():
            pass_on(lat_away + 2)

    finish(mesh_ref, w_out_ref, acc_ref, out_ref, joined_ref)

    @pl.loop(0, lat_count)
    def _(lat_away):
        lat = back(my_lat, lat_away, lat_count)

        @pl.loop(0, chips)
        def _(away):
            core_copy(shard_ref, lat_away, lat, away, chip, core).wait_send()

        @pl.loop(1, chips)
        def _(away):
            chip_copy(shard_ref, lat_away, lat, away, chip).wait_send()

    @pl.loop(1, lat_count)
    def _(away):
        column_copy(away, my_lat).wait_send()

    @pl.loop(1, devices)
    def _(away):
        slot_copy(away, me).wait_send()


def local(
    mesh_nodes,
    norm_gain,
    w_query,
    w_node_kv,
    obs_rows,
    w_obs_kv,
    obs_owner,
    neighbours,
    neighbour_mask,
    disk_tokens,
    w_disk_kv,
    disk_start,
    disk_extent,
    w_out,
):
    node_count, width = mesh_nodes.shape
    lon_count = lax.axis_size("lon")
    device_count = lax.axis_size("lat") * lon_count
    lat_count = lax.axis_size("lat")
    token_count, disk_count, token_width = disk_tokens.shape
    obs_count, row_width = obs_rows.shape
    capacity = 2 * obs_count // device_count
    slot_count = device_count * capacity
    vmem = pl.BlockSpec(memory_space=pltpu.VMEM)
    smem = pl.BlockSpec(memory_space=pltpu.SMEM)
    hbm = pl.BlockSpec(memory_space=pl.ANY)
    state = (HEADS, node_count, LANES)
    shard_count = lat_count * lon_count // 2
    dma = pltpu.SemaphoreType.DMA
    keys = device_count * token_count * disk_count // lat_count
    return pl.pallas_call(
        functools.partial(exchange_kernel, lat_count, lon_count),
        out_shape=jax.ShapeDtypeStruct((node_count, width), jnp.bfloat16),
        in_specs=[smem] * 2 + [vmem] * 11 + [hbm],
        out_specs=vmem,
        scratch_shapes=[
            pltpu.VMEM(state, jnp.bfloat16),
            pltpu.VMEM(state, jnp.float32),
            pltpu.VMEM(state, jnp.float32),
            pltpu.VMEM((device_count, disk_count, token_count, token_width), jnp.bfloat16),
            pltpu.VMEM((HEADS // 2, keys, LANES), jnp.bfloat16),
            pltpu.VMEM((HEADS, keys, LANES), jnp.bfloat16),
            pltpu.VMEM((node_count, width), jnp.bfloat16),
            pltpu.VMEM((device_count, capacity, row_width), jnp.bfloat16),
            pltpu.VMEM((device_count, capacity, row_width), jnp.bfloat16),
            pltpu.VMEM((slot_count, row_width), jnp.bfloat16),
            pltpu.VMEM((slot_count, node_count), jnp.float32),
            pltpu.VMEM((node_count, slot_count), jnp.float32),
            pltpu.VMEM((HEADS // 2, slot_count, LANES), jnp.bfloat16),
            pltpu.VMEM((HEADS, slot_count, LANES), jnp.bfloat16),
            dma,
            dma((lat_count,)),
            dma((lat_count,)),
            dma((shard_count,)),
            dma((shard_count,)),
            dma((shard_count,)),
            dma((shard_count,)),
            dma((device_count,)),
            dma((device_count,)),
        ],
        compiler_params=pltpu.CompilerParams(
            vmem_limit_bytes=VMEM_BYTES, collective_id=0, has_side_effects=True
        ),
        name="exchange",
    )(
        disk_start,
        disk_extent,
        mesh_nodes,
        norm_gain.reshape(1, width),
        w_query,
        w_node_kv,
        neighbours.T,
        neighbour_mask.T,
        obs_owner.reshape(1, obs_count),
        obs_rows,
        w_obs_kv,
        w_disk_kv,
        w_out,
        jnp.transpose(disk_tokens, (1, 0, 2)),
    )


def solution(mesh):
    rows = P(("lat", "lon"), None)
    return jax.shard_map(
        local,
        mesh=mesh,
        in_specs=(
            rows,
            P(),
            P(),
            P(),
            rows,
            P(),
            rows,
            rows,
            rows,
            P(("lat", "lon"), None, None),
            P(),
            P(),
            P(),
            P(),
        ),
        out_specs=rows,
        check_vma=False,
    )
```
